256 devices in a mesh: row: 8 (over y, x_hi), col: 32 (over z, x_lo, core).
Axes of the slice: x: 4 (x_hi: 2, x_lo: 2; x = x_hi * 2 + x_lo), y: 4, z: 8, core: 2. Of those that a mesh axis runs over, the one named last changes fastest.
Arguments:
- grad: bfloat16 [5120, 25600], P('row', 'col'), may hold values from -0.015625 to 0.015625
- momentum: float32 [5120, 25600], P('row', 'col'), may hold values from -0.0546875 to 0.0546875
Outputs:
- momentum_next: float32 [5120, 25600], P('row', 'col')
- update: bfloat16 [5120, 25600], P('row', 'col')
The draws below stay inside these ranges and needn't reach their ends.
All inputs are finite; a program needn't handle non-finite values.
Results may differ from the reference program's by a relative error of at most 0.023.
Values may be sent and summed in bfloat16 or wider, within the bound.
No kernel may reach another device: no remote copies, remote signals or barrier semaphores. Data moves between devices by JAX's collectives and lax.ppermute only.
A program may use at most 64 MiB of HBM per device.

```python
import math
import jax
import jax.numpy as jnp
from jax import lax

D = 5120
FF = 25600
N_COL = 32


def block_scale(rng, extent, pieces, least, largest):
    level = 1.0
    for dim, blocks in pieces:
        steps = jax.random.uniform(jax.random.fold_in(jax.random.fold_in(rng, 6), dim), (blocks,), jnp.float32, least / len(pieces), largest / len(pieces))
        level = level * jnp.repeat(jnp.exp(steps), extent[dim] // blocks).reshape((-1,) + (1,) * (len(extent) - 1 - dim))
    return level


def bell_draw(rng, extent, spread, most, shards=(), kind=jnp.bfloat16):
    factor_of = block_scale(rng, extent, shards, -0.22, 0.18) if shards else 1.0
    result = jax.random.normal(rng, extent, jnp.float32) * spread * factor_of
    return jnp.minimum(jnp.maximum(result, -most), most).astype(kind)


def setup_inputs(seed: int = 0) -> dict:
    seeds = jax.random.split(jax.random.key(seed), 3)
    return {
        "grad": bell_draw(seeds[0], (D, FF), (0.27 / (D ** 0.5 + FF ** 0.5)), 0.015625, ((0, 8), (1, 32))),
        "momentum": bell_draw(seeds[1], (D, FF), (0.9 / (D ** 0.5 + FF ** 0.5)), 0.0546875, ((0, 8), (1, 32)), jnp.float32),
    }


MOMENTUM_DECAY = 0.95
COEF_A = 3.4445
COEF_B = -4.775
COEF_C = 2.0315

def reference(grad, momentum):
    momentum_next = MOMENTUM_DECAY * momentum + grad.astype(jnp.float32)
    current = (grad.astype(jnp.float32) + MOMENTUM_DECAY * momentum_next).astype(jnp.bfloat16)
    block_width = FF // N_COL
    column_blocks = current.reshape(D, N_COL, block_width).transpose(1, 0, 2)

    def add_block(running, column_block):
        partial_gram = jnp.dot(column_block, column_block.T, preferred_element_type=jnp.float32)
        rounded = lax.optimization_barrier(partial_gram.astype(jnp.bfloat16))
        return (running + rounded.astype(jnp.float32), None)
    running, _ = lax.scan(add_block, jnp.zeros((D, D), jnp.float32), column_blocks)
    gram_matrix = running.astype(jnp.bfloat16)
    square = jnp.dot(gram_matrix, gram_matrix, preferred_element_type=jnp.float32)
    polynomial = (COEF_B * gram_matrix.astype(jnp.float32) + COEF_C * square).astype(jnp.bfloat16)
    product = jnp.dot(polynomial, current, preferred_element_type=jnp.float32)
    final_scale = 0.2 * math.sqrt(max(D, FF))
    update = (final_scale * (COEF_A * current.astype(jnp.float32) + product)).astype(jnp.bfloat16)
    return (momentum_next, update)
```

```python
import math

import jax
import jax.numpy as jnp
from jax import lax
from jax.sharding import PartitionSpec as P

D = 5120
FF = 25600


MOMENTUM_DECAY = 0.95
COEF_A = 3.4445
COEF_B = -4.775
COEF_C = 2.0315

AXES = ("row", "col")


def device_index(y, xh, z, xl, k):
    return ((y % 4) * 2 + xh) * 32 + (z % 8) * 4 + xl * 2 + k


def permutation(target):
    pairs = []
    for y in range(4):
        for xh in range(2):
            for z in range(8):
                for xl in range(2):
                    for k in range(2):
                        at = (y, xh, z, xl, k)
                        pairs.append((device_index(*at), device_index(*target(*at))))
    return pairs


CORE = permutation(lambda y, xh, z, xl, k: (y, xh, z, xl, 1 - k))
X_LO = permutation(lambda y, xh, z, xl, k: (y, xh, z, 1 - xl, k))
X_HI = permutation(lambda y, xh, z, xl, k: (y, 1 - xh, z, xl, k))
Y_UP = permutation(lambda y, xh, z, xl, k: (y + 1, xh, z, xl, k))
Y_DOWN = permutation(lambda y, xh, z, xl, k: (y - 1, xh, z, xl, k))
Y_TWO = permutation(lambda y, xh, z, xl, k: (y + 2, xh, z, xl, k))
Z_UP = permutation(lambda y, xh, z, xl, k: (y, xh, z + 1, xl, k))
Z_DOWN = permutation(lambda y, xh, z, xl, k: (y, xh, z - 1, xl, k))
X_STAY = permutation(lambda y, xh, z, xl, k: (y, k, z, xl, xh))
X_CROSS = permutation(lambda y, xh, z, xl, k: (y, k, z, 1 - xl, xh))
Z_GROUPS = [[z * 4 + q for z in range(8)] for q in range(4)]


def send(value, pairs):
    return lax.ppermute(value, AXES, pairs)


def gather_col(own, place):
    rows, width = own.shape
    z, xl, k = place
    full = jnp.zeros((4, 2, 2, 2, rows, width), own.dtype)

    def put(full, mine, other_xl, distance):
        zz = lax.rem(z + distance + 8, 8)
        pair = jnp.where(xl == 0, jnp.stack([mine, other_xl]), jnp.stack([other_xl, mine]))
        swapped = send(pair, CORE)
        both = jnp.where(k == 0, jnp.stack([pair, swapped]), jnp.stack([swapped, pair]))
        return lax.dynamic_update_slice(
            full, both[None, :, None], (zz // 2, 0, lax.rem(zz, 2), 0, 0, 0)
        )

    half = rows // 2
    up1, down1 = send(own, Z_UP), send(own, Z_DOWN)
    x0 = send(own, X_LO)
    up2, down2 = send(up1, Z_UP), send(down1, Z_DOWN)
    x1 = send(jnp.stack([up1, down1]), X_LO)
    up3, down3 = send(up2, Z_UP), send(down2, Z_DOWN)
    x2 = send(jnp.stack([up2, down2]), X_LO)
    up4, down4 = send(up3[:half], Z_UP), send(down3[half:], Z_DOWN)
    x3u, x3d = send(x2[0], Z_UP), send(x2[1], Z_DOWN)
    far = jnp.concatenate([up4, down4], 0)
    x4 = send(far, X_LO)
    full = put(full, own, x0, 0)
    full = put(full, up1, x1[0], -1)
    full = put(full, down1, x1[1], 1)
    full = put(full, up2, x2[0], -2)
    full = put(full, down2, x2[1], 2)
    full = put(full, up3, x3u, -3)
    full = put(full, down3, x3d, 3)
    full = put(full, far, x4, 4)
    return full.reshape(32 * rows, width)


def on_device(grad, momentum):
    momentum_next = MOMENTUM_DECAY * momentum + grad.astype(jnp.float32)
    current = (grad.astype(jnp.float32) + MOMENTUM_DECAY * momentum_next).astype(jnp.bfloat16)
    n, m = current.shape
    row, col = lax.axis_index("row"), lax.axis_index("col")
    y, xh = row // 2, lax.rem(row, 2)
    z, xl, k = col // 4, lax.rem(col // 2, 2), lax.rem(col, 2)
    place = (z, xl, k)

    with jax.named_scope("rows"):
        below, above = send(current, Y_UP), send(current, Y_DOWN)
        beside = send(current, X_HI)
        across = send(current, Y_TWO)

    with jax.named_scope("gram"):
        same = k == xh
        mine = jnp.where(same, current, beside)
        other = send(jnp.where(same, beside, current), CORE)

        def tile(block):
            swapped = send(block, CORE)
            first = jnp.einsum("rc,sc->rs", block, mine, preferred_element_type=jnp.float32)
            second = jnp.einsum("rc,sc->rs", swapped, other, preferred_element_type=jnp.float32)
            return (first + second).astype(jnp.bfloat16)

        partial = jnp.zeros((4, n, n), jnp.bfloat16)
        for block, shift in ((current, 0), (below, 3), (above, 1), (across, 2)):
            partial = lax.dynamic_update_slice(
                partial, tile(block)[None], (lax.rem(y + shift, 4), 0, 0)
            )
        partial = partial.reshape(4 * n, n)

    with jax.named_scope("reduce"):
        beside_late, partial = lax.optimization_barrier((beside, partial))
        part = lax.psum_scatter(
            partial, "col", scatter_dimension=0, tiled=True, axis_index_groups=Z_GROUPS
        )
        quarter = n // 4
        stay = lax.dynamic_slice(part, (xl * quarter, 0), (quarter, n))
        cross = lax.dynamic_slice(part, ((1 - xl) * quarter, 0), (quarter, n))
        owned = (
            send(stay, X_STAY).astype(jnp.float32) + send(cross, X_CROSS).astype(jnp.float32)
        ).astype(jnp.bfloat16)

    with jax.named_scope("slab"):
        slab = jnp.zeros((4, 2, n, m), jnp.bfloat16)
        for block, shift in ((current, 0), (below, 3), (above, 1), (across, 2)):
            slab = lax.dynamic_update_slice(
                slab, block[None, None], (lax.rem(y + shift, 4), xh, 0, 0)
            )
        rest = (
            (beside_late, 0),
            (send(beside_late, Y_UP), 3),
            (send(beside_late, Y_DOWN), 1),
            (send(beside_late, Y_TWO), 2),
        )
        for block, shift in rest:
            slab = lax.dynamic_update_slice(
                slab, block[None, None], (lax.rem(y + shift, 4), 1 - xh, 0, 0)
            )
        slab = slab.reshape(8 * n, m)

    with jax.named_scope("gram_rows"):
        owned_beside = send(owned, X_HI)
        pair = jnp.where(
            xh == 0,
            jnp.concatenate([owned, owned_beside], 1),
            jnp.concatenate([owned_beside, owned], 1),
        )
        gram_rows = jnp.zeros((quarter, 8 * n), jnp.bfloat16)
        for block, shift in (
            (pair, 0),
            (send(pair, Y_UP), 3),
            (send(pair, Y_DOWN), 1),
            (send(pair, Y_TWO), 2),
        ):
            gram_rows = lax.dynamic_update_slice(
                gram_rows, block, (0, lax.rem(y + shift, 4) * (2 * n))
            )

    with jax.named_scope("gram_cols"):
        gram_cols = gather_col(owned, place)
    with jax.named_scope("poly"):
        square = jnp.dot(gram_rows, gram_cols, preferred_element_type=jnp.float32)
        polynomial = (COEF_B * owned.astype(jnp.float32) + COEF_C * square).astype(jnp.bfloat16)
    with jax.named_scope("poly_cols"):
        poly_cols = gather_col(polynomial, place)
    with jax.named_scope("product"):
        product = jnp.einsum("kr,kc->rc", poly_cols, slab, preferred_element_type=jnp.float32)
        final_scale = 0.2 * math.sqrt(max(D, FF))
        update = (final_scale * (COEF_A * current.astype(jnp.float32) + product)).astype(
            jnp.bfloat16
        )
    return (momentum_next, update)


def solution(mesh):
    placed = (P("row", "col"), P("row", "col"))
    return jax.shard_map(
        on_device,
        mesh=mesh,
        in_specs=placed,
        out_specs=(P("row", "col"), P("row", "col")),
        check_vma=False,
    )
```

```python
import math

import jax
import jax.numpy as jnp
from jax import lax
from jax.experimental import pallas as pl
from jax.experimental.pallas import tpu as pltpu
from jax.sharding import PartitionSpec as P

D = 5120
FF = 25600


MOMENTUM_DECAY = 0.95
COEF_A = 3.4445
COEF_B = -4.775
COEF_C = 2.0315

AXES = ("row", "col")


def device_index(y, xh, z, xl, k):
    return ((y % 4) * 2 + xh) * 32 + (z % 8) * 4 + xl * 2 + k


def permutation(target):
    pairs = []
    for y in range(4):
        for xh in range(2):
            for z in range(8):
                for xl in range(2):
                    for k in range(2):
                        at = (y, xh, z, xl, k)
                        pairs.append((device_index(*at), device_index(*target(*at))))
    return pairs


CORE = permutation(lambda y, xh, z, xl, k: (y, xh, z, xl, 1 - k))
X_LO = permutation(lambda y, xh, z, xl, k: (y, xh, z, 1 - xl, k))
X_HI = permutation(lambda y, xh, z, xl, k: (y, 1 - xh, z, xl, k))
Y_UP = permutation(lambda y, xh, z, xl, k: (y + 1, xh, z, xl, k))
Y_DOWN = permutation(lambda y, xh, z, xl, k: (y - 1, xh, z, xl, k))
Z_UP = permutation(lambda y, xh, z, xl, k: (y, xh, z + 1, xl, k))
Z_DOWN = permutation(lambda y, xh, z, xl, k: (y, xh, z - 1, xl, k))
X_STAY = permutation(lambda y, xh, z, xl, k: (y, k, z, xl, xh))
X_CROSS = permutation(lambda y, xh, z, xl, k: (y, k, z, 1 - xl, xh))
Y_GROUPS = [[y * 2 + xh for y in range(4)] for xh in range(2)]
Z_GROUPS = [[z * 4 + q for z in range(8)] for q in range(4)]


def send(value, pairs):
    return lax.ppermute(value, AXES, pairs)


def fence(*values):
    return lax.optimization_barrier(values)


def gather_col(own, swap, aside, use_near):
    rows = own.shape[0]
    half = rows // 2
    exchange = (lambda value: send(value, CORE)) if swap else (lambda value: None)
    up1, down1 = send(own, Z_UP), send(own, Z_DOWN)
    x0 = send(own, X_LO)
    own_swap = exchange(own)
    up1, down1 = fence(up1, down1)

    up2, down2 = send(up1, Z_UP), send(down1, Z_DOWN)
    u1 = jnp.concatenate([up1, down1], 0)
    x1 = send(u1, X_LO)
    u1_swap = exchange(u1)
    up2, down2, x0, aside = fence(up2, down2, x0, aside)

    up3, down3 = send(up2, Z_UP), send(down2, Z_DOWN)
    u2 = jnp.concatenate([up2, down2], 0)
    x2 = send(u2, X_LO)
    x0_swap, u2_swap = exchange(x0), exchange(u2)
    up3, down3, x1 = fence(up3, down3, x1)

    up4, down4 = send(up3[:half], Z_UP), send(down3[half:], Z_DOWN)
    u3 = jnp.concatenate([up3, down3], 0)
    u3_swap, x1_swap = exchange(u3), exchange(x1)
    up4, down4, x2 = fence(up4, down4, x2)

    u4 = jnp.concatenate([up4, down4], 0)
    x4 = send(u4, X_LO)
    u4_swap = exchange(u4)
    x3u, x3d = send(x2[:rows], Z_UP), send(x2[rows:], Z_DOWN)
    x2_swap = exchange(x2)

    def both(value, swapped, zs):
        found = [(value, [(d, 0) for d in zs])]
        return found + ([(swapped, [(d, 1) for d in zs])] if swap else [])

    near = both(own, own_swap, (0,)) + both(u1, u1_swap, (-1, 1)) + both(u2, u2_swap, (-2, 2))
    near += both(u3, u3_swap, (-3, 3)) + both(u4, u4_swap, (4,))
    used = use_near(near, aside)
    x3u, x3d, x4, used = fence(x3u, x3d, x4, used)
    far = both(x0, x0_swap, (0,)) + both(x1, x1_swap, (-1, 1)) + both(x2, x2_swap, (-2, 2))
    far += both(x3u, exchange(x3u), (-3,)) + both(x3d, exchange(x3d), (3,))
    far += both(x4, exchange(x4), (4,))
    return far, used


def place_pieces(scratch, refs, tables, at_ref, n, cores):
    z, k = at_ref[2], at_ref[4]
    quarter, eighth = n // 4, n // 8
    for ref, table in zip(refs, tables):
        for i, (d, other_core) in enumerate(table):
            zz = lax.rem(z + (d + 8), 8)
            for j in range(2):
                block = j
                if cores == 2:
                    block = 2 * j + (1 - k if other_core else k)
                start = pl.multiple_of(block * n + zz * eighth, 16)
                scratch[pl.ds(start, eighth), :] = ref[
                    i * quarter + j * eighth : i * quarter + (j + 1) * eighth, :
                ]


def write_tile(at, count, block, swapped, mine, other, partial):
    m, n = mine.shape
    parts = block + swapped
    of_each = len(block)

    def kernel(*refs):
        mine_ref, other_ref, out_ref = refs[len(parts)], refs[len(parts) + 1], refs[-1]
        total = None
        for i, ref in enumerate(refs[: len(parts)]):
            against = mine_ref if i < of_each else other_ref
            rows = ref.shape[0]
            start = (i % of_each) * rows
            term = lax.dot_general(
                ref[...],
                against[start : start + rows, :],
                (((0,), (0,)), ((), ())),
                preferred_element_type=jnp.float32,
            )
            total = term if total is None else total + term
        total = total.astype(out_ref.dtype)
        out_ref[:, 0] = total.reshape(out_ref.shape[0], *out_ref.shape[2:])

    operands = parts + [mine, other]
    in_specs = [pl.BlockSpec(value.shape, lambda i: (0, 0)) for value in operands]
    aliases = {}
    if partial is not None:
        aliases = {len(operands): 0}
        operands.append(partial)
        in_specs.append(pl.BlockSpec(memory_space=pl.ANY))
    return pl.pallas_call(
        kernel,
        out_shape=jax.ShapeDtypeStruct((8, count, n // 8, n), jnp.bfloat16),
        grid=(1,),
        in_specs=in_specs,
        out_specs=pl.BlockSpec((8, 1, n // 8, n), lambda i: (0, at, 0, 0)),
        input_output_aliases=aliases,
        cost_estimate=pl.CostEstimate(
            flops=4 * n * n * m, bytes_accessed=8 * n * m + 2 * n * n, transcendentals=0
        ),
        compiler_params=pltpu.CompilerParams(vmem_limit_bytes=18 * 1024 * 1024),
        name="gram_tile",
    )(*operands)


def local_call(kernel, out_shape, operands, scratch_shapes, flops, limit, name):
    in_specs = [pl.BlockSpec(memory_space=pltpu.SMEM)]
    in_specs += [pl.BlockSpec(memory_space=pltpu.VMEM)] * (len(operands) - 1)
    return pl.pallas_call(
        kernel,
        out_shape=out_shape,
        in_specs=in_specs,
        out_specs=jax.tree.map(lambda _: pl.BlockSpec(memory_space=pltpu.VMEM), out_shape),
        scratch_shapes=scratch_shapes,
        cost_estimate=pl.CostEstimate(
            flops=flops,
            bytes_accessed=sum(value.size * value.dtype.itemsize for value in operands),
            transcendentals=0,
        ),
        compiler_params=pltpu.CompilerParams(vmem_limit_bytes=limit * 1024 * 1024),
        name=name,
    )(*operands)


def square_rows(place_at, part, rows, pieces, total):
    _, both_rows, n = rows.shape
    tables = [table for _, table in pieces]
    values = [value for value, _ in pieces]
    count = len(values)

    def kernel(at_ref, rows_ref, *refs):
        piece_refs, scratch = refs[:count], refs[-1]
        xl = at_ref[3] if part == 0 else 1 - at_ref[3]
        place_pieces(scratch, piece_refs, tables, at_ref, n, 1)
        result = None if part == 0 else refs[count][...]
        for j in range(2):
            term = jnp.dot(
                rows_ref[2 * xl + j],
                scratch[j * n : (j + 1) * n, :],
                preferred_element_type=jnp.float32,
            )
            result = term if result is None else result + term
        if part == 0:
            refs[count][...] = result
        else:
            same = at_ref[1] == at_ref[4]
            here, beside = result[: both_rows // 2], result[both_rows // 2 :]
            refs[count + 1][...] = jnp.where(same, here, beside)
            refs[count + 2][...] = jnp.where(same, beside, here)

    operands = [place_at, rows] + values
    if part == 0:
        out_shape = jax.ShapeDtypeStruct((both_rows, n), jnp.float32)
    else:
        operands.append(total)
        out_shape = (jax.ShapeDtypeStruct((both_rows // 2, n), jnp.float32),) * 2
    scratch_shapes = [pltpu.VMEM((2 * n, n), jnp.bfloat16)]
    flops = 4 * both_rows * n * n
    return local_call(kernel, out_shape, operands, scratch_shapes, flops, 16, "square_rows")


def product_cols(place_at, part, blocks, pieces, total, scale):
    m, n = blocks[0][0].shape
    tables = [table for _, table in pieces]
    values = [value for value, _ in pieces]
    count = len(values)

    def kernel(at_ref, *refs):
        block_refs, piece_refs = refs[:8], refs[8 : 8 + count]
        out_ref, scratch, sum_ref = refs[-3:]
        y, xh = at_ref[0], at_ref[1]
        xl = at_ref[3] if part == 0 else 1 - at_ref[3]
        place_pieces(scratch, piece_refs, tables, at_ref, n, 2)
        if part == 0:
            sum_ref[...] = jnp.zeros_like(sum_ref)
        else:
            sum_ref[...] = refs[8 + count][...]
        for i in range(4):
            yy = lax.rem(y + blocks[2 * i][1], 4)

            @pl.when(yy // 2 == xl)
            def _(i=i, yy=yy):
                terms = []
                for side in range(2):
                    xx = 1 - xh if side else xh
                    start = pl.multiple_of((2 * lax.rem(yy, 2) + xx) * n, 16)
                    terms.append(
                        jnp.dot(
                            block_refs[2 * i + side][...],
                            scratch[pl.ds(start, n), :],
                            preferred_element_type=jnp.float32,
                        )
                    )
                sum_ref[...] += terms[0] + terms[1]

        if part == 0:
            out_ref[...] = sum_ref[...]
        else:
            own = block_refs[0][...].astype(jnp.float32)
            out_ref[...] = (scale * (COEF_A * own + sum_ref[...])).astype(out_ref.dtype)

    operands = [place_at] + [block for block, _ in blocks] + values
    operands += [] if part == 0 else [total]
    out_shape = jax.ShapeDtypeStruct((m, n), jnp.float32 if part == 0 else jnp.bfloat16)
    scratch_shapes = [pltpu.VMEM((4 * n, n), jnp.bfloat16), pltpu.VMEM((m, n), jnp.float32)]
    flops = 8 * m * n * n
    return local_call(kernel, out_shape, operands, scratch_shapes, flops, 28, "product_cols")


def on_device(grad, momentum):
    grad, momentum = grad.T, momentum.T
    m, n = grad.shape
    quarter, eighth = n // 4, n // 8
    row, col = lax.axis_index("row"), lax.axis_index("col")
    y, xh = row // 2, lax.rem(row, 2)
    z, xl, k = col // 4, lax.rem(col // 2, 2), lax.rem(col, 2)
    same = k == xh
    place_at = jnp.stack([y, xh, z, xl, k]).astype(jnp.int32)

    def next_momentum(grad, momentum):
        return MOMENTUM_DECAY * momentum + grad.astype(jnp.float32)

    current = (
        grad.astype(jnp.float32) + MOMENTUM_DECAY * next_momentum(grad, momentum)
    ).astype(jnp.bfloat16)

    def around(block):
        below, above = send(block, Y_UP), send(block, Y_DOWN)
        return below, above, [send(below[: m // 2], Y_UP), send(above[m // 2 :], Y_DOWN)]

    with jax.named_scope("rows"):
        below, above, across = around(current)
        beside = send(current, X_HI)
        current_swap = send(current, CORE)
        mine = jnp.where(same, current, beside)
        other = send(jnp.where(same, beside, current), CORE)

    with jax.named_scope("gram"):
        partial = write_tile(0, 4, [current], [current_swap], mine, other, None)
        partial = write_tile(1, 4, [below], [send(below, CORE)], mine, other, partial)
        partial = write_tile(2, 4, [above], [send(above, CORE)], mine, other, partial)
        partial, across[0], across[1] = fence(partial, across[0], across[1])
        across_swap = [send(value, CORE) for value in across]
        partial = write_tile(3, 4, across, across_swap, mine, other, partial)

    with jax.named_scope("reduce"):
        part = lax.psum_scatter(
            partial.reshape(32 * eighth, n),
            "col",
            scatter_dimension=0,
            tiled=True,
            axis_index_groups=Z_GROUPS,
        ).reshape(4, eighth, n)
        late, grad, momentum, across[0] = fence(beside, grad, momentum, across[0])
        late_below, late_above, late_across = around(late)
        late_across = jnp.concatenate(late_across, 0)
        across = jnp.concatenate(across, 0)
        momentum_next = next_momentum(grad, momentum)
        part, late, late_below, late_above, late_across, across, momentum_next = fence(
            part, late, late_below, late_above, late_across, across, momentum_next
        )
        by_shift = (part[0], part[2], part[3], part[1])

        def rows_of(which):
            at = lax.rem(2 * which - y + 4, 4)
            return jnp.concatenate(
                [lax.select_n(at, *by_shift), lax.select_n(lax.rem(at + 1, 4), *by_shift)], 0
            )

        def add(first, second):
            return (first.astype(jnp.float32) + second.astype(jnp.float32)).astype(jnp.bfloat16)

        stay, cross = rows_of(xl), rows_of(1 - xl)
        owned = add(send(stay, X_STAY), send(cross, X_CROSS))
        own_rows = add(stay, send(cross, X_LO))

    def first_square(pieces, beside_rows):
        rows = lax.all_gather(
            jnp.concatenate([own_rows, beside_rows], 0),
            "row",
            axis=0,
            axis_index_groups=Y_GROUPS,
        )
        return rows, square_rows(place_at, 0, rows, pieces, None)

    with jax.named_scope("gram_cols"):
        pieces, (rows, square) = gather_col(owned, False, send(own_rows, X_HI), first_square)
    with jax.named_scope("poly"):
        square, square_other = square_rows(place_at, 1, rows, pieces, square)
        square += send(square_other, CORE)
        polynomial = (COEF_B * owned.astype(jnp.float32) + COEF_C * square).astype(jnp.bfloat16)

    scale = 0.2 * math.sqrt(max(D, FF))

    blocks = (
        (current, 0),
        (late, 0),
        (below, 3),
        (late_below, 3),
        (above, 1),
        (late_above, 1),
        (across, 2),
        (late_across, 2),
    )

    def first_product(pieces, _):
        return product_cols(place_at, 0, blocks, pieces, None, scale)

    with jax.named_scope("poly_cols"):
        pieces, product = gather_col(polynomial, True, None, first_product)
    with jax.named_scope("product"):
        update = product_cols(place_at, 1, blocks, pieces, product, scale)
    return (momentum_next.T, update.T)


def solution(mesh):
    placed = (P("row", "col"), P("row", "col"))
    return jax.shard_map(
        on_device,
        mesh=mesh,
        in_specs=placed,
        out_specs=(P("row", "col"), P("row", "col")),
        check_vma=False,
    )
```

```python
import math

import jax
import jax.numpy as jnp
from jax import lax
from jax.experimental import pallas as pl
from jax.experimental.pallas import tpu as pltpu
from jax.sharding import PartitionSpec as P

D = 5120
FF = 25600


MOMENTUM_DECAY = 0.95
COEF_A = 3.4445
COEF_B = -4.775
COEF_C = 2.0315

AXES = ("row", "col")


def device_index(y, xh, z, xl, k):
    return ((y % 4) * 2 + xh) * 32 + (z % 8) * 4 + xl * 2 + k


def permutation(target):
    pairs = []
    for y in range(4):
        for xh in range(2):
            for z in range(8):
                for xl in range(2):
                    for k in range(2):
                        at = (y, xh, z, xl, k)
                        pairs.append((device_index(*at), device_index(*target(*at))))
    return pairs


CORE = permutation(lambda y, xh, z, xl, k: (y, xh, z, xl, 1 - k))
X_LO = permutation(lambda y, xh, z, xl, k: (y, xh, z, 1 - xl, k))
X_HI = permutation(lambda y, xh, z, xl, k: (y, 1 - xh, z, xl, k))
Y_UP = permutation(lambda y, xh, z, xl, k: (y + 1, xh, z, xl, k))
Y_DOWN = permutation(lambda y, xh, z, xl, k: (y - 1, xh, z, xl, k))
Z_UP = permutation(lambda y, xh, z, xl, k: (y, xh, z + 1, xl, k))
Z_DOWN = permutation(lambda y, xh, z, xl, k: (y, xh, z - 1, xl, k))
X_FAR = permutation(lambda y, xh, z, xl, k: (y, 1 - xh, z, 1 - xl, k))
X_STAY = permutation(lambda y, xh, z, xl, k: (y, k, z, xl, xh))
X_CROSS = permutation(lambda y, xh, z, xl, k: (y, k, z, 1 - xl, xh))
Y_GROUPS = [[y * 2 + xh for y in range(4)] for xh in range(2)]
Z_GROUPS = [[z * 4 + q for z in range(8)] for q in range(4)]


def send(value, pairs):
    return lax.ppermute(value, AXES, pairs)


def fence(*values):
    return lax.optimization_barrier(values)


def gather_col(own, swap, aside, use_near):
    rows = own.shape[0]
    half = rows // 2
    exchange = (lambda value: send(value, CORE)) if swap else (lambda value: None)
    up1, down1 = send(own, Z_UP), send(own, Z_DOWN)
    x0 = send(own, X_LO)
    own_swap = exchange(own)
    if swap:
        up1, down1, x0 = fence(up1, down1, x0)
    else:
        up1, down1, aside = fence(up1, down1, aside)

    up2, down2 = send(up1, Z_UP), send(down1, Z_DOWN)
    u1 = jnp.concatenate([up1, down1], 0)
    x1 = send(u1, X_LO)
    x0_swap = exchange(x0)
    up2, down2, x0, own_swap, x0_swap = fence(up2, down2, x0, own_swap, x0_swap)

    up3, down3 = send(up2, Z_UP), send(down2, Z_DOWN)
    u2 = jnp.concatenate([up2, down2], 0)
    x2 = send(u2, X_LO)
    u1_swap = exchange(u1)
    up3, down3, x1, u1_swap = fence(up3, down3, x1, u1_swap)

    up4, down4 = send(up3[:half], Z_UP), send(down3[half:], Z_DOWN)
    u3 = jnp.concatenate([up3, down3], 0)
    u2_swap, x1_swap = exchange(u2), exchange(x1)
    up4, down4, x2, u2_swap, x1_swap = fence(up4, down4, x2, u2_swap, x1_swap)

    u4 = jnp.concatenate([up4, down4], 0)
    x4 = send(u4, X_LO)
    u3_swap, u4_swap = exchange(u3), exchange(u4)
    x3u, x3d = send(x2[:rows], Z_UP), send(x2[rows:], Z_DOWN)
    x2_swap = exchange(x2)

    def both(value, swapped, zs):
        found = [(value, [(d, 0) for d in zs])]
        return found + ([(swapped, [(d, 1) for d in zs])] if swap else [])

    near = both(own, own_swap, (0,)) + both(u1, u1_swap, (-1, 1)) + both(u2, u2_swap, (-2, 2))
    near += both(u3, u3_swap, (-3, 3)) + both(u4, u4_swap, (4,))
    used = use_near(near, aside)
    x3u, x3d, x4, used = fence(x3u, x3d, x4, used)
    far = both(x0, x0_swap, (0,)) + both(x1, x1_swap, (-1, 1)) + both(x2, x2_swap, (-2, 2))
    far += both(x3u, exchange(x3u), (-3,)) + both(x3d, exchange(x3d), (3,))
    far += both(x4, exchange(x4), (4,))
    return far, used


def place_pieces(scratch, refs, tables, at_ref, n, cores):
    xh, z, k = at_ref[1], at_ref[2], at_ref[4]
    side = jnp.where(xh == k, 0, 1)
    quarter, eighth = n // 4, n // 8
    for ref, table in zip(refs, tables):
        for i, (d, other_core) in enumerate(table):
            zz = lax.rem(z + (d + 8), 8)
            for j in range(2):
                block = j
                if cores == 2:
                    block = 2 * j + (1 - side if other_core else side)
                start = pl.multiple_of(block * n + zz * eighth, 16)
                scratch[pl.ds(start, eighth), :] = ref[
                    i * quarter + j * eighth : i * quarter + (j + 1) * eighth, :
                ]


def write_tile(at, count, block, swapped, mine, other, partial):
    m, n = mine.shape
    parts = block + swapped
    of_each = len(block)

    def kernel(*refs):
        mine_ref, other_ref, out_ref = refs[len(parts)], refs[len(parts) + 1], refs[-1]
        total = None
        for i, ref in enumerate(refs[: len(parts)]):
            against = mine_ref if i < of_each else other_ref
            rows = ref.shape[0]
            start = (i % of_each) * rows
            term = lax.dot_general(
                ref[...],
                against[start : start + rows, :],
                (((0,), (0,)), ((), ())),
                preferred_element_type=jnp.float32,
            )
            total = term if total is None else total + term
        total = total.astype(out_ref.dtype)
        out_ref[:, 0] = total.reshape(out_ref.shape[0], *out_ref.shape[2:])

    operands = parts + [mine, other]
    in_specs = [pl.BlockSpec(value.shape, lambda i: (0, 0)) for value in operands]
    aliases = {}
    if partial is not None:
        aliases = {len(operands): 0}
        operands.append(partial)
        in_specs.append(pl.BlockSpec(memory_space=pl.ANY))
    return pl.pallas_call(
        kernel,
        out_shape=jax.ShapeDtypeStruct((8, count, n // 8, n), jnp.bfloat16),
        grid=(1,),
        in_specs=in_specs,
        out_specs=pl.BlockSpec((8, 1, n // 8, n), lambda i: (0, at, 0, 0)),
        input_output_aliases=aliases,
        cost_estimate=pl.CostEstimate(
            flops=4 * n * n * m, bytes_accessed=8 * n * m + 2 * n * n, transcendentals=0
        ),
        compiler_params=pltpu.CompilerParams(vmem_limit_bytes=18 * 1024 * 1024),
        name="gram_tile",
    )(*operands)


def local_call(kernel, out_shape, operands, scratch_shapes, flops, limit, name):
    in_specs = [pl.BlockSpec(memory_space=pltpu.SMEM)]
    in_specs += [pl.BlockSpec(memory_space=pltpu.VMEM)] * (len(operands) - 1)
    return pl.pallas_call(
        kernel,
        out_shape=out_shape,
        in_specs=in_specs,
        out_specs=jax.tree.map(lambda _: pl.BlockSpec(memory_space=pltpu.VMEM), out_shape),
        scratch_shapes=scratch_shapes,
        cost_estimate=pl.CostEstimate(
            flops=flops,
            bytes_accessed=sum(value.size * value.dtype.itemsize for value in operands),
            transcendentals=0,
        ),
        compiler_params=pltpu.CompilerParams(vmem_limit_bytes=limit * 1024 * 1024),
        name=name,
    )(*operands)


def square_rows(place_at, part, rows, pieces, total):
    _, both_rows, n = rows.shape
    tables = [table for _, table in pieces]
    values = [value for value, _ in pieces]
    count = len(values)

    def kernel(at_ref, rows_ref, *refs):
        piece_refs, scratch = refs[:count], refs[-1]
        xl = at_ref[3] if part == 0 else 1 - at_ref[3]
        place_pieces(scratch, piece_refs, tables, at_ref, n, 1)
        result = None if part == 0 else refs[count][...]
        for j in range(2):
            term = jnp.dot(
                rows_ref[2 * xl + j],
                scratch[j * n : (j + 1) * n, :],
                preferred_element_type=jnp.float32,
            )
            result = term if result is None else result + term
        if part == 0:
            refs[count][...] = result
        else:
            same = at_ref[1] == at_ref[4]
            here, beside = result[: both_rows // 2], result[both_rows // 2 :]
            refs[count + 1][...] = jnp.where(same, here, beside)
            refs[count + 2][...] = jnp.where(same, beside, here)

    operands = [place_at, rows] + values
    if part == 0:
        out_shape = jax.ShapeDtypeStruct((both_rows, n), jnp.float32)
    else:
        operands.append(total)
        out_shape = (jax.ShapeDtypeStruct((both_rows // 2, n), jnp.float32),) * 2
    scratch_shapes = [pltpu.VMEM((2 * n, n), jnp.bfloat16)]
    flops = 4 * both_rows * n * n
    return local_call(kernel, out_shape, operands, scratch_shapes, flops, 16, "square_rows")


def product_cols(place_at, part, blocks, pieces, total, scale):
    m, wide = blocks[0].shape
    n = wide // 2
    tables = [table for _, table in pieces]
    values = [value for value, _ in pieces]
    count = len(values)

    def kernel(at_ref, *refs):
        block_refs, piece_refs = refs[:4], refs[4 : 4 + count]
        out_ref, scratch = refs[-2:]
        y = at_ref[0]
        xl = at_ref[3] if part == 0 else 1 - at_ref[3]
        place_pieces(scratch, piece_refs, tables, at_ref, n, 2)
        by_shift = (block_refs[0], block_refs[2], block_refs[3], block_refs[1])
        for shift in range(4):

            @pl.when(lax.rem(2 * xl - y + 4, 4) == shift)
            def _(shift=shift):
                result = None if part == 0 else refs[4 + count][...]
                for j in range(2):
                    term = jnp.dot(
                        by_shift[(shift + j) % 4][...],
                        scratch[j * wide : (j + 1) * wide, :],
                        preferred_element_type=jnp.float32,
                    )
                    result = term if result is None else result + term
                if part == 1:
                    own = block_refs[0][:, :n].astype(jnp.float32)
                    result = scale * (COEF_A * own + result)
                out_ref[...] = result.astype(out_ref.dtype)

    operands = [place_at] + list(blocks) + values
    operands += [] if part == 0 else [total]
    out_shape = jax.ShapeDtypeStruct((m, n), jnp.float32 if part == 0 else jnp.bfloat16)
    scratch_shapes = [pltpu.VMEM((4 * n, n), jnp.bfloat16)]
    flops = 8 * m * n * n
    return local_call(kernel, out_shape, operands, scratch_shapes, flops, 28, "product_cols")


def on_device(grad, momentum):
    grad, momentum = grad.T, momentum.T
    m, n = grad.shape
    quarter, eighth = n // 4, n // 8
    row, col = lax.axis_index("row"), lax.axis_index("col")
    y, xh = row // 2, lax.rem(row, 2)
    z, xl, k = col // 4, lax.rem(col // 2, 2), lax.rem(col, 2)
    same = k == xh
    place_at = jnp.stack([y, xh, z, xl, k]).astype(jnp.int32)

    def next_momentum(grad, momentum):
        return MOMENTUM_DECAY * momentum + grad.astype(jnp.float32)

    current = (
        grad.astype(jnp.float32) + MOMENTUM_DECAY * next_momentum(grad, momentum)
    ).astype(jnp.bfloat16)

    def around(block):
        below, above = send(block, Y_UP), send(block, Y_DOWN)
        return below, above, [send(below[: m // 2], Y_UP), send(above[m // 2 :], Y_DOWN)]

    with jax.named_scope("rows"):
        below, above, across = around(current)
        beside = send(current, X_HI)
        current_swap = send(current, CORE)
        mine = jnp.where(same, current, beside)
        other = send(jnp.where(same, beside, current), CORE)

    with jax.named_scope("gram"):
        partial = write_tile(0, 4, [current], [current_swap], mine, other, None)
        partial = write_tile(1, 4, [below], [send(below, CORE)], mine, other, partial)
        partial = write_tile(2, 4, [above], [send(above, CORE)], mine, other, partial)
        partial, across[0], across[1] = fence(partial, across[0], across[1])
        across_swap = [send(value, CORE) for value in across]
        partial = write_tile(3, 4, across, across_swap, mine, other, partial)

    with jax.named_scope("reduce"):
        part = lax.psum_scatter(
            partial.reshape(32 * eighth, n),
            "col",
            scatter_dimension=0,
            tiled=True,
            axis_index_groups=Z_GROUPS,
        ).reshape(4, eighth, n)
        late, grad, momentum, across[0] = fence(beside, grad, momentum, across[0])
        late_below, late_above, late_across = around(late)
        momentum_next = next_momentum(grad, momentum)

        def beside_each_other(first, second):
            return jnp.concatenate([first, second], 1)

        def by_halves(parts, late_parts):
            return jnp.concatenate(
                [beside_each_other(*halves) for halves in zip(parts, late_parts)], 0
            )

        blocks = (
            beside_each_other(current, late),
            beside_each_other(below, late_below),
            beside_each_other(above, late_above),
            by_halves(across, late_across),
        )
        part, blocks, momentum_next = fence(part, blocks, momentum_next)
        by_shift = (part[0], part[2], part[3], part[1])

        def rows_of(which):
            at = lax.rem(2 * which - y + 4, 4)
            return jnp.concatenate(
                [lax.select_n(at, *by_shift), lax.select_n(lax.rem(at + 1, 4), *by_shift)], 0
            )

        def add(first, second):
            return (first.astype(jnp.float32) + second.astype(jnp.float32)).astype(jnp.bfloat16)

        stay, cross = rows_of(xl), rows_of(1 - xl)
        owned = add(send(stay, X_STAY), send(cross, X_CROSS))
        own_rows = add(stay, send(cross, X_LO))
        beside_rows = add(send(stay, X_HI), send(cross, X_FAR))
        both_rows = jnp.concatenate([own_rows, beside_rows], 0)

    def first_square(pieces, both_rows):
        rows = lax.all_gather(both_rows, "row", axis=0, axis_index_groups=Y_GROUPS)
        return rows, square_rows(place_at, 0, rows, pieces, None)

    with jax.named_scope("gram_cols"):
        pieces, (rows, square) = gather_col(owned, False, both_rows, first_square)
    with jax.named_scope("poly"):
        square, square_other = square_rows(place_at, 1, rows, pieces, square)
        square += send(square_other, CORE)
        polynomial = (COEF_B * owned.astype(jnp.float32) + COEF_C * square).astype(jnp.bfloat16)

    scale = 0.2 * math.sqrt(max(D, FF))

    def first_product(pieces, _):
        return product_cols(place_at, 0, blocks, pieces, None, scale)

    with jax.named_scope("poly_cols"):
        pieces, product = gather_col(polynomial, True, None, first_product)
    with jax.named_scope("product"):
        update = product_cols(place_at, 1, blocks, pieces, product, scale)
    return (momentum_next.T, update.T)


def solution(mesh):
    placed = (P("row", "col"), P("row", "col"))
    return jax.shard_map(
        on_device,
        mesh=mesh,
        in_specs=placed,
        out_specs=(P("row", "col"), P("row", "col")),
        check_vma=False,
    )
```

```python
import math

import jax
import jax.numpy as jnp
from jax import lax
from jax.experimental import pallas as pl
from jax.experimental.pallas import tpu as pltpu
from jax.sharding import PartitionSpec as P

D = 5120
FF = 25600


MOMENTUM_DECAY = 0.95
COEF_A = 3.4445
COEF_B = -4.775
COEF_C = 2.0315

AXES = ("row", "col")


def device_index(y, xh, z, xl, k):
    return ((y % 4) * 2 + xh) * 32 + (z % 8) * 4 + xl * 2 + k


def permutation(target):
    pairs = []
    for y in range(4):
        for xh in range(2):
            for z in range(8):
                for xl in range(2):
                    for k in range(2):
                        at = (y, xh, z, xl, k)
                        pairs.append((device_index(*at), device_index(*target(*at))))
    return pairs


CORE = permutation(lambda y, xh, z, xl, k: (y, xh, z, xl, 1 - k))
X_LO = permutation(lambda y, xh, z, xl, k: (y, xh, z, 1 - xl, k))
X_HI = permutation(lambda y, xh, z, xl, k: (y, 1 - xh, z, xl, k))
Y_UP = permutation(lambda y, xh, z, xl, k: (y + 1, xh, z, xl, k))
Y_DOWN = permutation(lambda y, xh, z, xl, k: (y - 1, xh, z, xl, k))
Z_UP = permutation(lambda y, xh, z, xl, k: (y, xh, z + 1, xl, k))
Z_DOWN = permutation(lambda y, xh, z, xl, k: (y, xh, z - 1, xl, k))
X_FAR = permutation(lambda y, xh, z, xl, k: (y, 1 - xh, z, 1 - xl, k))
X_STAY = permutation(lambda y, xh, z, xl, k: (y, k, z, xl, xh))
X_CROSS = permutation(lambda y, xh, z, xl, k: (y, k, z, 1 - xl, xh))
Y_GROUPS = [[y * 2 + xh for y in range(4)] for xh in range(2)]
Z_GROUPS = [[z * 4 + q for z in range(8)] for q in range(4)]


def send(value, pairs):
    return lax.ppermute(value, AXES, pairs)


def fence(*values):
    return lax.optimization_barrier(values)


def gather_col(own, swap, aside, use_near):
    rows = own.shape[0]
    half = rows // 2
    exchange = (lambda value: send(value, CORE)) if swap else (lambda value: None)
    up1, down1 = send(own, Z_UP), send(own, Z_DOWN)
    x0 = send(own, X_LO)
    own_swap = exchange(own)
    if swap:
        up1, down1, x0 = fence(up1, down1, x0)
    else:
        up1, down1, aside = fence(up1, down1, aside)

    up2, down2 = send(up1, Z_UP), send(down1, Z_DOWN)
    u1 = jnp.concatenate([up1, down1], 0)
    x1 = send(u1, X_LO)
    x0_swap = exchange(x0)
    up2, down2, x0, own_swap, x0_swap = fence(up2, down2, x0, own_swap, x0_swap)

    up3, down3 = send(up2, Z_UP), send(down2, Z_DOWN)
    u2 = jnp.concatenate([up2, down2], 0)
    x2 = send(u2, X_LO)
    u1_swap = exchange(u1)
    up3, down3, u1_swap = fence(up3, down3, u1_swap)

    up4, down4 = send(up3[:half], Z_UP), send(down3[half:], Z_DOWN)
    u3 = jnp.concatenate([up3, down3], 0)
    u2_swap = exchange(u2)
    up4, down4, x1, x2, u2_swap = fence(up4, down4, x1, x2, u2_swap)
    x1_swap = exchange(x1)

    u4 = jnp.concatenate([up4, down4], 0)
    x4 = send(u4, X_LO)
    u3_swap, u4_swap = exchange(u3), exchange(u4)
    x3u, x3d = send(x2[:rows], Z_UP), send(x2[rows:], Z_DOWN)
    x2_swap = exchange(x2)

    def both(value, swapped, zs):
        found = [(value, [(d, 0) for d in zs])]
        return found + ([(swapped, [(d, 1) for d in zs])] if swap else [])

    near = both(own, own_swap, (0,)) + both(u1, u1_swap, (-1, 1)) + both(u2, u2_swap, (-2, 2))
    near += both(u3, u3_swap, (-3, 3)) + both(u4, u4_swap, (4,))
    used = use_near(near, aside)
    x3u, x3d, x4, used = fence(x3u, x3d, x4, used)
    far = both(x0, x0_swap, (0,)) + both(x1, x1_swap, (-1, 1)) + both(x2, x2_swap, (-2, 2))
    far += both(x3u, exchange(x3u), (-3,)) + both(x3d, exchange(x3d), (3,))
    far += both(x4, exchange(x4), (4,))
    return far, used


def place_pieces(scratch, refs, tables, at_ref, n, cores):
    xh, z, k = at_ref[1], at_ref[2], at_ref[4]
    side = jnp.where(xh == k, 0, 1)
    quarter, eighth = n // 4, n // 8
    for ref, table in zip(refs, tables):
        for i, (d, other_core) in enumerate(table):
            zz = lax.rem(z + (d + 8), 8)
            for j in range(2):
                block = j
                if cores == 2:
                    block = 2 * j + (1 - side if other_core else side)
                start = pl.multiple_of(block * n + zz * eighth, 16)
                scratch[pl.ds(start, eighth), :] = ref[
                    i * quarter + j * eighth : i * quarter + (j + 1) * eighth, :
                ]


def first_half_tile(block, mine):
    m, n = mine.shape

    def kernel(*refs):
        out_ref = refs[-1]
        out_ref[...] = against_parts(refs[: len(block)], refs[len(block)])

    return pl.pallas_call(
        kernel,
        out_shape=jax.ShapeDtypeStruct((n, n), jnp.float32),
        cost_estimate=pl.CostEstimate(
            flops=2 * n * n * m, bytes_accessed=4 * n * m + 4 * n * n, transcendentals=0
        ),
        compiler_params=pltpu.CompilerParams(vmem_limit_bytes=16 * 1024 * 1024),
        name="first_half_tile",
    )(*block, mine)


def against_parts(refs, against_ref):
    total = None
    for i, ref in enumerate(refs):
        rows = ref.shape[0]
        term = lax.dot_general(
            ref[...],
            against_ref[i * rows : (i + 1) * rows, :],
            (((0,), (0,)), ((), ())),
            preferred_element_type=jnp.float32,
        )
        total = term if total is None else total + term
    return total


def write_tile(at, count, block, swapped, mine, other, partial, half=None):
    m, n = mine.shape
    count_swapped, count_block = len(swapped), len(block)

    def kernel(*refs):
        out_ref = refs[-1]
        total = against_parts(refs[:count_swapped], refs[count_swapped])
        if half is None:
            own = refs[count_swapped + 1 : count_swapped + 1 + count_block]
            total += against_parts(own, refs[count_swapped + 1 + count_block])
        else:
            total += refs[count_swapped + 1][...]
        total = total.astype(out_ref.dtype)
        out_ref[:, 0] = total.reshape(out_ref.shape[0], *out_ref.shape[2:])

    operands = swapped + [other] + (block + [mine] if half is None else [half])
    in_specs = [pl.BlockSpec(value.shape, lambda i: (0, 0)) for value in operands]
    aliases = {}
    if partial is not None:
        aliases = {len(operands): 0}
        operands.append(partial)
        in_specs.append(pl.BlockSpec(memory_space=pl.ANY))
    return pl.pallas_call(
        kernel,
        out_shape=jax.ShapeDtypeStruct((8, count, n // 8, n), jnp.bfloat16),
        grid=(1,),
        in_specs=in_specs,
        out_specs=pl.BlockSpec((8, 1, n // 8, n), lambda i: (0, at, 0, 0)),
        input_output_aliases=aliases,
        cost_estimate=pl.CostEstimate(
            flops=4 * n * n * m, bytes_accessed=8 * n * m + 2 * n * n, transcendentals=0
        ),
        compiler_params=pltpu.CompilerParams(vmem_limit_bytes=18 * 1024 * 1024),
        name="gram_tile",
    )(*operands)


def local_call(kernel, out_shape, operands, scratch_shapes, flops, limit, name):
    in_specs = [pl.BlockSpec(memory_space=pltpu.SMEM)]
    in_specs += [pl.BlockSpec(memory_space=pltpu.VMEM)] * (len(operands) - 1)
    return pl.pallas_call(
        kernel,
        out_shape=out_shape,
        in_specs=in_specs,
        out_specs=jax.tree.map(lambda _: pl.BlockSpec(memory_space=pltpu.VMEM), out_shape),
        scratch_shapes=scratch_shapes,
        cost_estimate=pl.CostEstimate(
            flops=flops,
            bytes_accessed=sum(value.size * value.dtype.itemsize for value in operands),
            transcendentals=0,
        ),
        compiler_params=pltpu.CompilerParams(vmem_limit_bytes=limit * 1024 * 1024),
        name=name,
    )(*operands)


def square_rows(place_at, part, rows, pieces, total):
    _, both_rows, n = rows.shape
    tables = [table for _, table in pieces]
    values = [value for value, _ in pieces]
    count = len(values)

    def kernel(at_ref, rows_ref, *refs):
        piece_refs, scratch = refs[:count], refs[-1]
        xl = at_ref[3] if part == 0 else 1 - at_ref[3]
        place_pieces(scratch, piece_refs, tables, at_ref, n, 1)
        result = None if part == 0 else refs[count][...]
        for j in range(2):
            term = jnp.dot(
                rows_ref[2 * xl + j],
                scratch[j * n : (j + 1) * n, :],
                preferred_element_type=jnp.float32,
            )
            result = term if result is None else result + term
        if part == 0:
            refs[count][...] = result
        else:
            same = at_ref[1] == at_ref[4]
            here, beside = result[: both_rows // 2], result[both_rows // 2 :]
            refs[count + 1][...] = jnp.where(same, here, beside)
            refs[count + 2][...] = jnp.where(same, beside, here)

    operands = [place_at, rows] + values
    if part == 0:
        out_shape = jax.ShapeDtypeStruct((both_rows, n), jnp.float32)
    else:
        operands.append(total)
        out_shape = (jax.ShapeDtypeStruct((both_rows // 2, n), jnp.float32),) * 2
    scratch_shapes = [pltpu.VMEM((2 * n, n), jnp.bfloat16)]
    flops = 4 * both_rows * n * n
    return local_call(kernel, out_shape, operands, scratch_shapes, flops, 16, "square_rows")


def product_cols(place_at, part, blocks, pieces, total, scale):
    m, wide = blocks[0].shape
    n = wide // 2
    tables = [table for _, table in pieces]
    values = [value for value, _ in pieces]
    count = len(values)

    def kernel(at_ref, *refs):
        block_refs, piece_refs = refs[:4], refs[4 : 4 + count]
        out_ref, scratch = refs[-2:]
        y = at_ref[0]
        xl = at_ref[3] if part == 0 else 1 - at_ref[3]
        place_pieces(scratch, piece_refs, tables, at_ref, n, 2)
        by_shift = (block_refs[0], block_refs[2], block_refs[3], block_refs[1])
        for shift in range(4):

            @pl.when(lax.rem(2 * xl - y + 4, 4) == shift)
            def _(shift=shift):
                result = None if part == 0 else refs[4 + count][...]
                for j in range(2):
                    term = jnp.dot(
                        by_shift[(shift + j) % 4][...],
                        scratch[j * wide : (j + 1) * wide, :],
                        preferred_element_type=jnp.float32,
                    )
                    result = term if result is None else result + term
                if part == 1:
                    own = block_refs[0][:, :n].astype(jnp.float32)
                    result = scale * (COEF_A * own + result)
                out_ref[...] = result.astype(out_ref.dtype)

    operands = [place_at] + list(blocks) + values
    operands += [] if part == 0 else [total]
    out_shape = jax.ShapeDtypeStruct((m, n), jnp.float32 if part == 0 else jnp.bfloat16)
    scratch_shapes = [pltpu.VMEM((4 * n, n), jnp.bfloat16)]
    flops = 8 * m * n * n
    return local_call(kernel, out_shape, operands, scratch_shapes, flops, 28, "product_cols")


def on_device(grad, momentum):
    grad, momentum = grad.T, momentum.T
    m, n = grad.shape
    quarter, eighth = n // 4, n // 8
    row, col = lax.axis_index("row"), lax.axis_index("col")
    y, xh = row // 2, lax.rem(row, 2)
    z, xl, k = col // 4, lax.rem(col // 2, 2), lax.rem(col, 2)
    same = k == xh
    place_at = jnp.stack([y, xh, z, xl, k]).astype(jnp.int32)

    def next_momentum(grad, momentum):
        return MOMENTUM_DECAY * momentum + grad.astype(jnp.float32)

    current = (
        grad.astype(jnp.float32) + MOMENTUM_DECAY * next_momentum(grad, momentum)
    ).astype(jnp.bfloat16)

    def around(block):
        below, above = send(block, Y_UP), send(block, Y_DOWN)
        return below, above, [send(below[: m // 2], Y_UP), send(above[m // 2 :], Y_DOWN)]

    with jax.named_scope("rows"):
        below, above, across = around(current)
        beside = send(current, X_HI)
        current_swap = send(current, CORE)
        mine = jnp.where(same, current, beside)
        other = send(jnp.where(same, beside, current), CORE)

    with jax.named_scope("gram"):
        partial = write_tile(0, 4, [current], [current_swap], mine, other, None)
        partial = write_tile(1, 4, [below], [send(below, CORE)], mine, other, partial)
        partial = write_tile(2, 4, [above], [send(above, CORE)], mine, other, partial)
        partial, across[0], across[1] = fence(partial, across[0], across[1])
        across_swap = [send(value, CORE) for value in across]
        half = first_half_tile(across, mine)
        partial = write_tile(3, 4, across, across_swap, mine, other, partial, half)

    with jax.named_scope("reduce"):
        part = lax.psum_scatter(
            partial.reshape(32 * eighth, n),
            "col",
            scatter_dimension=0,
            tiled=True,
            axis_index_groups=Z_GROUPS,
        ).reshape(4, eighth, n)
        late, grad, momentum, across[0] = fence(beside, grad, momentum, across[0])
        late_below, late_above, late_across = around(late)
        momentum_next = next_momentum(grad, momentum)

        def beside_each_other(first, second):
            return jnp.concatenate([first, second], 1)

        def by_halves(parts, late_parts):
            return jnp.concatenate(
                [beside_each_other(*halves) for halves in zip(parts, late_parts)], 0
            )

        blocks = (
            beside_each_other(current, late),
            beside_each_other(below, late_below),
            beside_each_other(above, late_above),
            by_halves(across, late_across),
        )
        part, blocks, momentum_next = fence(part, blocks, momentum_next)
        by_shift = (part[0], part[2], part[3], part[1])

        def rows_of(which):
            at = lax.rem(2 * which - y + 4, 4)
            return jnp.concatenate(
                [lax.select_n(at, *by_shift), lax.select_n(lax.rem(at + 1, 4), *by_shift)], 0
            )

        def add(first, second):
            return (first.astype(jnp.float32) + second.astype(jnp.float32)).astype(jnp.bfloat16)

        stay, cross = rows_of(xl), rows_of(1 - xl)
        owned = add(send(stay, X_STAY), send(cross, X_CROSS))
        own_rows = add(stay, send(cross, X_LO))
        beside_rows = add(send(stay, X_HI), send(cross, X_FAR))
        both_rows = jnp.concatenate([own_rows, beside_rows], 0)

    def first_square(pieces, both_rows):
        rows = lax.all_gather(both_rows, "row", axis=0, axis_index_groups=Y_GROUPS)
        return rows, square_rows(place_at, 0, rows, pieces, None)

    with jax.named_scope("gram_cols"):
        pieces, (rows, square) = gather_col(owned, False, both_rows, first_square)
    with jax.named_scope("poly"):
        square, square_other = square_rows(place_at, 1, rows, pieces, square)
        square += send(square_other, CORE)
        polynomial = (COEF_B * owned.astype(jnp.float32) + COEF_C * square).astype(jnp.bfloat16)

    scale = 0.2 * math.sqrt(max(D, FF))

    def first_product(pieces, _):
        return product_cols(place_at, 0, blocks, pieces, None, scale)

    with jax.named_scope("poly_cols"):
        pieces, product = gather_col(polynomial, True, None, first_product)
    with jax.named_scope("product"):
        update = product_cols(place_at, 1, blocks, pieces, product, scale)
    return (momentum_next.T, update.T)


def solution(mesh):
    placed = (P("row", "col"), P("row", "col"))
    return jax.shard_map(
        on_device,
        mesh=mesh,
        in_specs=placed,
        out_specs=(P("row", "col"), P("row", "col")),
        check_vma=False,
    )
```

```python
import math

import jax
import jax.numpy as jnp
from jax import lax
from jax.experimental import pallas as pl
from jax.experimental.pallas import tpu as pltpu
from jax.sharding import PartitionSpec as P

D = 5120
FF = 25600


MOMENTUM_DECAY = 0.95
COEF_A = 3.4445
COEF_B = -4.775
COEF_C = 2.0315

AXES = ("row", "col")


def device_index(y, xh, z, xl, k):
    return ((y % 4) * 2 + xh) * 32 + (z % 8) * 4 + xl * 2 + k


def permutation(target):
    pairs = []
    for y in range(4):
        for xh in range(2):
            for z in range(8):
                for xl in range(2):
                    for k in range(2):
                        at = (y, xh, z, xl, k)
                        pairs.append((device_index(*at), device_index(*target(*at))))
    return pairs


CORE = permutation(lambda y, xh, z, xl, k: (y, xh, z, xl, 1 - k))
X_LO = permutation(lambda y, xh, z, xl, k: (y, xh, z, 1 - xl, k))
X_HI = permutation(lambda y, xh, z, xl, k: (y, 1 - xh, z, xl, k))
Y_UP = permutation(lambda y, xh, z, xl, k: (y + 1, xh, z, xl, k))
Y_DOWN = permutation(lambda y, xh, z, xl, k: (y - 1, xh, z, xl, k))
Z_UP = permutation(lambda y, xh, z, xl, k: (y, xh, z + 1, xl, k))
Z_DOWN = permutation(lambda y, xh, z, xl, k: (y, xh, z - 1, xl, k))
X_FAR = permutation(lambda y, xh, z, xl, k: (y, 1 - xh, z, 1 - xl, k))


def cores_where(pairs, same):
    return [pair for pair in pairs if (pair[0] % 2 == pair[0] // 32 % 2) == same]


X_LO_OFF = cores_where(X_LO, False)
X_HI_ON = cores_where(X_HI, True)
X_FAR_ON = cores_where(X_FAR, True)
X_STAY = permutation(lambda y, xh, z, xl, k: (y, k, z, xl, xh))
X_CROSS = permutation(lambda y, xh, z, xl, k: (y, k, z, 1 - xl, xh))
Y_GROUPS = [[y * 2 + xh for y in range(4)] for xh in range(2)]
Z_GROUPS = [[z * 4 + q for z in range(8)] for q in range(4)]


def send(value, pairs):
    return lax.ppermute(value, AXES, pairs)


def fence(*values):
    return lax.optimization_barrier(values)


def gather_col(own, swap, aside, use_near):
    rows = own.shape[0]
    half = rows // 2
    exchange = (lambda value: send(value, CORE)) if swap else (lambda value: None)
    up1, down1 = send(own, Z_UP), send(own, Z_DOWN)
    x0 = send(own, X_LO)
    own_swap = exchange(own)
    if swap:
        up1, down1, x0 = fence(up1, down1, x0)
    else:
        up1, down1, aside = fence(up1, down1, aside)

    up2, down2 = send(up1, Z_UP), send(down1, Z_DOWN)
    u1 = jnp.concatenate([up1, down1], 0)
    x1 = send(u1, X_LO)
    x0_swap = exchange(x0)
    up2, down2, x0, own_swap, x0_swap = fence(up2, down2, x0, own_swap, x0_swap)

    up3, down3 = send(up2, Z_UP), send(down2, Z_DOWN)
    u2 = jnp.concatenate([up2, down2], 0)
    x2 = send(u2, X_LO)
    u1_swap = exchange(u1)
    up3, down3, u1_swap = fence(up3, down3, u1_swap)

    up4, down4 = send(up3[:half], Z_UP), send(down3[half:], Z_DOWN)
    u3 = jnp.concatenate([up3, down3], 0)
    u2_swap = exchange(u2)
    up4, down4, x1, x2, u2_swap = fence(up4, down4, x1, x2, u2_swap)
    x1_swap = exchange(x1)

    u4 = jnp.concatenate([up4, down4], 0)
    x4 = send(u4, X_LO)
    u3_swap, u4_swap = exchange(u3), exchange(u4)
    x3u, x3d = send(x2[:rows], Z_UP), send(x2[rows:], Z_DOWN)
    x2_swap = exchange(x2)

    def both(value, swapped, zs):
        found = [(value, [(d, 0) for d in zs])]
        return found + ([(swapped, [(d, 1) for d in zs])] if swap else [])

    near = both(own, own_swap, (0,)) + both(u1, u1_swap, (-1, 1)) + both(u2, u2_swap, (-2, 2))
    near += both(u3, u3_swap, (-3, 3)) + both(u4, u4_swap, (4,))
    used = use_near(near, aside)
    x3u, x3d, x4, used = fence(x3u, x3d, x4, used)
    far = both(x0, x0_swap, (0,)) + both(x1, x1_swap, (-1, 1)) + both(x2, x2_swap, (-2, 2))
    far += both(x3u, exchange(x3u), (-3,)) + both(x3d, exchange(x3d), (3,))
    far += both(x4, exchange(x4), (4,))
    return far, used


def place_pieces(scratch, refs, tables, at_ref, n, cores):
    xh, z, k = at_ref[1], at_ref[2], at_ref[4]
    side = jnp.where(xh == k, 0, 1)
    quarter, eighth = n // 4, n // 8
    for ref, table in zip(refs, tables):
        for i, (d, other_core) in enumerate(table):
            zz = lax.rem(z + (d + 8), 8)
            for j in range(2):
                block = j
                if cores == 2:
                    block = 2 * j + (1 - side if other_core else side)
                start = pl.multiple_of(block * n + zz * eighth, 16)
                scratch[pl.ds(start, eighth), :] = ref[
                    i * quarter + j * eighth : i * quarter + (j + 1) * eighth, :
                ]


def first_half_tile(block, mine):
    m, n = mine.shape

    def kernel(*refs):
        out_ref = refs[-1]
        out_ref[...] = against_parts(refs[: len(block)], refs[len(block)])

    return pl.pallas_call(
        kernel,
        out_shape=jax.ShapeDtypeStruct((n, n), jnp.float32),
        cost_estimate=pl.CostEstimate(
            flops=2 * n * n * m, bytes_accessed=4 * n * m + 4 * n * n, transcendentals=0
        ),
        compiler_params=pltpu.CompilerParams(vmem_limit_bytes=16 * 1024 * 1024),
        name="first_half_tile",
    )(*block, mine)


def against_parts(refs, against_ref):
    total = None
    for i, ref in enumerate(refs):
        rows = ref.shape[0]
        term = lax.dot_general(
            ref[...],
            against_ref[i * rows : (i + 1) * rows, :],
            (((0,), (0,)), ((), ())),
            preferred_element_type=jnp.float32,
        )
        total = term if total is None else total + term
    return total


def write_tile(at, count, block, swapped, mine, other, partial, half=None):
    m, n = mine.shape
    count_swapped, count_block = len(swapped), len(block)

    def kernel(*refs):
        out_ref = refs[-1]
        total = against_parts(refs[:count_swapped], refs[count_swapped])
        if half is None:
            own = refs[count_swapped + 1 : count_swapped + 1 + count_block]
            total += against_parts(own, refs[count_swapped + 1 + count_block])
        else:
            total += refs[count_swapped + 1][...]
        total = total.astype(out_ref.dtype)
        out_ref[:, 0] = total.reshape(out_ref.shape[0], *out_ref.shape[2:])

    operands = swapped + [other] + (block + [mine] if half is None else [half])
    in_specs = [pl.BlockSpec(value.shape, lambda i: (0, 0)) for value in operands]
    aliases = {}
    if partial is not None:
        aliases = {len(operands): 0}
        operands.append(partial)
        in_specs.append(pl.BlockSpec(memory_space=pl.ANY))
    return pl.pallas_call(
        kernel,
        out_shape=jax.ShapeDtypeStruct((8, count, n // 8, n), jnp.bfloat16),
        grid=(1,),
        in_specs=in_specs,
        out_specs=pl.BlockSpec((8, 1, n // 8, n), lambda i: (0, at, 0, 0)),
        input_output_aliases=aliases,
        cost_estimate=pl.CostEstimate(
            flops=4 * n * n * m, bytes_accessed=8 * n * m + 2 * n * n, transcendentals=0
        ),
        compiler_params=pltpu.CompilerParams(vmem_limit_bytes=18 * 1024 * 1024),
        name="gram_tile",
    )(*operands)


def local_call(kernel, out_shape, operands, scratch_shapes, flops, limit, name):
    in_specs = [pl.BlockSpec(memory_space=pltpu.SMEM)]
    in_specs += [pl.BlockSpec(memory_space=pltpu.VMEM)] * (len(operands) - 1)
    return pl.pallas_call(
        kernel,
        out_shape=out_shape,
        in_specs=in_specs,
        out_specs=jax.tree.map(lambda _: pl.BlockSpec(memory_space=pltpu.VMEM), out_shape),
        scratch_shapes=scratch_shapes,
        cost_estimate=pl.CostEstimate(
            flops=flops,
            bytes_accessed=sum(value.size * value.dtype.itemsize for value in operands),
            transcendentals=0,
        ),
        compiler_params=pltpu.CompilerParams(vmem_limit_bytes=limit * 1024 * 1024),
        name=name,
    )(*operands)


def square_rows(place_at, part, rows, pieces, total):
    _, both_rows, n = rows.shape
    tables = [table for _, table in pieces]
    values = [value for value, _ in pieces]
    count = len(values)

    def kernel(at_ref, rows_ref, *refs):
        piece_refs, scratch = refs[:count], refs[-1]
        xl = at_ref[3] if part == 0 else 1 - at_ref[3]
        place_pieces(scratch, piece_refs, tables, at_ref, n, 1)
        result = None if part == 0 else refs[count][...]
        for j in range(2):
            term = jnp.dot(
                rows_ref[2 * xl + j],
                scratch[j * n : (j + 1) * n, :],
                preferred_element_type=jnp.float32,
            )
            result = term if result is None else result + term
        if part == 0:
            refs[count][...] = result
        else:
            same = at_ref[1] == at_ref[4]
            here, beside = result[: both_rows // 2], result[both_rows // 2 :]
            refs[count + 1][...] = jnp.where(same, here, beside)
            refs[count + 2][...] = jnp.where(same, beside, here)

    operands = [place_at, rows] + values
    if part == 0:
        out_shape = jax.ShapeDtypeStruct((both_rows, n), jnp.float32)
    else:
        operands.append(total)
        out_shape = (jax.ShapeDtypeStruct((both_rows // 2, n), jnp.float32),) * 2
    scratch_shapes = [pltpu.VMEM((2 * n, n), jnp.bfloat16)]
    flops = 4 * both_rows * n * n
    return local_call(kernel, out_shape, operands, scratch_shapes, flops, 16, "square_rows")


def product_cols(place_at, part, blocks, pieces, total, scale):
    m, wide = blocks[0].shape
    n = wide // 2
    tables = [table for _, table in pieces]
    values = [value for value, _ in pieces]
    count = len(values)

    def kernel(at_ref, *refs):
        block_refs, piece_refs = refs[:4], refs[4 : 4 + count]
        out_ref, scratch = refs[-2:]
        y = at_ref[0]
        xl = at_ref[3] if part == 0 else 1 - at_ref[3]
        place_pieces(scratch, piece_refs, tables, at_ref, n, 2)
        by_shift = (block_refs[0], block_refs[2], block_refs[3], block_refs[1])
        for shift in range(4):

            @pl.when(lax.rem(2 * xl - y + 4, 4) == shift)
            def _(shift=shift):
                result = None if part == 0 else refs[4 + count][...]
                for j in range(2):
                    term = jnp.dot(
                        by_shift[(shift + j) % 4][...],
                        scratch[j * wide : (j + 1) * wide, :],
                        preferred_element_type=jnp.float32,
                    )
                    result = term if result is None else result + term
                if part == 1:
                    own = block_refs[0][:, :n].astype(jnp.float32)
                    result = scale * (COEF_A * own + result)
                out_ref[...] = result.astype(out_ref.dtype)

    operands = [place_at] + list(blocks) + values
    operands += [] if part == 0 else [total]
    out_shape = jax.ShapeDtypeStruct((m, n), jnp.float32 if part == 0 else jnp.bfloat16)
    scratch_shapes = [pltpu.VMEM((4 * n, n), jnp.bfloat16)]
    flops = 8 * m * n * n
    return local_call(kernel, out_shape, operands, scratch_shapes, flops, 28, "product_cols")


def on_device(grad, momentum):
    grad, momentum = grad.T, momentum.T
    m, n = grad.shape
    quarter, eighth = n // 4, n // 8
    row, col = lax.axis_index("row"), lax.axis_index("col")
    y, xh = row // 2, lax.rem(row, 2)
    z, xl, k = col // 4, lax.rem(col // 2, 2), lax.rem(col, 2)
    same = k == xh
    place_at = jnp.stack([y, xh, z, xl, k]).astype(jnp.int32)

    def next_momentum(grad, momentum):
        return MOMENTUM_DECAY * momentum + grad.astype(jnp.float32)

    current = (
        grad.astype(jnp.float32) + MOMENTUM_DECAY * next_momentum(grad, momentum)
    ).astype(jnp.bfloat16)

    def around(block):
        below, above = send(block, Y_UP), send(block, Y_DOWN)
        return below, above, [send(below[: m // 2], Y_UP), send(above[m // 2 :], Y_DOWN)]

    with jax.named_scope("rows"):
        below, above, across = around(current)
        beside = send(current, X_HI)
        current_swap = send(current, CORE)
        mine = jnp.where(same, current, beside)
        other = send(jnp.where(same, beside, current), CORE)

    with jax.named_scope("gram"):
        partial = write_tile(0, 4, [current], [current_swap], mine, other, None)
        partial = write_tile(1, 4, [below], [send(below, CORE)], mine, other, partial)
        partial = write_tile(2, 4, [above], [send(above, CORE)], mine, other, partial)
        partial, across[0], across[1] = fence(partial, across[0], across[1])
        across_swap = [send(value, CORE) for value in across]
        half = first_half_tile(across, mine)
        partial = write_tile(3, 4, across, across_swap, mine, other, partial, half)

    with jax.named_scope("reduce"):
        part = lax.psum_scatter(
            partial.reshape(32 * eighth, n),
            "col",
            scatter_dimension=0,
            tiled=True,
            axis_index_groups=Z_GROUPS,
        ).reshape(4, eighth, n)
        late, grad, momentum, across[0] = fence(beside, grad, momentum, across[0])
        late_below, late_above, late_across = around(late)
        momentum_next = next_momentum(grad, momentum)

        def beside_each_other(first, second):
            return jnp.concatenate([first, second], 1)

        def by_halves(parts, late_parts):
            return jnp.concatenate(
                [beside_each_other(*halves) for halves in zip(parts, late_parts)], 0
            )

        blocks = (
            beside_each_other(current, late),
            beside_each_other(below, late_below),
            beside_each_other(above, late_above),
            by_halves(across, late_across),
        )
        part, blocks, momentum_next = fence(part, blocks, momentum_next)
        by_shift = (part[0], part[2], part[3], part[1])

        def rows_of(which):
            at = lax.rem(2 * which - y + 4, 4)
            return jnp.concatenate(
                [lax.select_n(at, *by_shift), lax.select_n(lax.rem(at + 1, 4), *by_shift)], 0
            )

        def add(first, second):
            return (first.astype(jnp.float32) + second.astype(jnp.float32)).astype(jnp.bfloat16)

        stay, cross = rows_of(xl), rows_of(1 - xl)
        owned = add(send(stay, X_STAY), send(cross, X_CROSS))
        own_rows = jnp.where(same, owned, add(stay, send(cross, X_LO_OFF)))
        beside_rows = add(send(stay, X_HI_ON), send(cross, X_FAR_ON))
        beside_rows = jnp.where(same, send(owned, CORE), beside_rows)
        both_rows = jnp.concatenate([own_rows, beside_rows], 0)

    def first_square(pieces, both_rows):
        rows = lax.all_gather(both_rows, "row", axis=0, axis_index_groups=Y_GROUPS)
        return rows, square_rows(place_at, 0, rows, pieces, None)

    with jax.named_scope("gram_cols"):
        pieces, (rows, square) = gather_col(owned, False, both_rows, first_square)
    with jax.named_scope("poly"):
        square, square_other = square_rows(place_at, 1, rows, pieces, square)
        square += send(square_other, CORE)
        polynomial = (COEF_B * owned.astype(jnp.float32) + COEF_C * square).astype(jnp.bfloat16)

    scale = 0.2 * math.sqrt(max(D, FF))

    def first_product(pieces, _):
        return product_cols(place_at, 0, blocks, pieces, None, scale)

    with jax.named_scope("poly_cols"):
        pieces, product = gather_col(polynomial, True, None, first_product)
    with jax.named_scope("product"):
        update = product_cols(place_at, 1, blocks, pieces, product, scale)
    return (momentum_next.T, update.T)


def solution(mesh):
    placed = (P("row", "col"), P("row", "col"))
    return jax.shard_map(
        on_device,
        mesh=mesh,
        in_specs=placed,
        out_specs=(P("row", "col"), P("row", "col")),
        check_vma=False,
    )
```
